256 devices in a mesh: tm: 4 (over z_hi), tile: 64 (over y, x, z_lo, core).
Axes of the slice: x: 4, y: 4, z: 8 (z_hi: 4, z_lo: 2; z = z_hi * 2 + z_lo), core: 2. Of those that a mesh axis runs over, the one named last changes fastest.
Arguments:
- frames: bfloat16 [1024, 49152], P('tm', 'tile'), may hold values from -16 to 16
- segments: int32 [1024], replicated, may hold values from 0 to 2, as said below
- offset: int32 [1], replicated, may hold values from 0 to 45056
Outputs:
- instant: float32 [4096, 49152], P('tm', 'tile')
- lagged: float32 [4096, 49152], P('tm', 'tile')
The draws below stay inside these ranges and needn't reach their ends.
Inputs may be any that keep to these rules, and one draw needn't show every extreme that they name: `segments`: each trajectory is a run of frames, in order of its id.
All inputs are finite; a program needn't handle non-finite values.
Results may differ from the reference program's by a relative error of at most 0.0036.
Values may be sent and summed in bfloat16 or wider, within the bound.
No kernel may reach another device: no remote copies, remote signals or barrier semaphores. Data moves between devices by JAX's collectives and lax.ppermute only.
A program may use at most 64 MiB of HBM per device.

```python
import math
import jax
import jax.numpy as jnp
from jax import lax

F = 49152
S = 4096
LAG = 256
FRAMES = 1024


def draw_frames(key, part):
    keys = jax.random.split(key, 7)
    times = jnp.arange(FRAMES, dtype=jnp.float32)[:, None]
    drift = jax.random.normal(keys[0], (1, F), jnp.float32)
    first_load = jax.random.normal(keys[1], (1, F), jnp.float32)
    second_load = jax.random.normal(keys[2], (1, F), jnp.float32)
    period = jax.random.uniform(keys[3], (), jnp.float32, 2.0 * LAG, 6.0 * LAG)
    phase = jax.random.uniform(keys[4], (), jnp.float32, -math.pi, math.pi)
    slow = 1.4 * jnp.cos(2.0 * math.pi * times / period + phase)
    rough = jax.random.normal(keys[5], (FRAMES, 1), jnp.float32)
    noise = jax.random.normal(keys[6], (FRAMES, F), jnp.float32)
    values = 0.8 * drift * (1.0 + 2.0 * times / FRAMES) + first_load * slow + 0.7 * second_load * rough + noise
    return jnp.clip(values, -16.0, 16.0).astype(jnp.bfloat16)


def draw_segments(key, part):
    keys = jax.random.split(jax.random.fold_in(key, 11), 2)
    first_end = jax.random.randint(keys[0], (), FRAMES // 8, FRAMES // 4, jnp.int32)
    second_end = jax.random.randint(keys[1], (), 5 * FRAMES // 8, 3 * FRAMES // 4, jnp.int32)
    stamps = jnp.arange(FRAMES, dtype=jnp.int32)
    return (stamps >= first_end).astype(jnp.int32) + (stamps >= second_end).astype(jnp.int32)


def setup_inputs(seed: int = 0) -> dict:
    seeds = jax.random.split(jax.random.key(seed), 4)
    return {
        "frames": draw_frames(jax.random.fold_in(seeds[3], 71), 0),
        "segments": draw_segments(jax.random.fold_in(seeds[3], 71), 0),
        "offset": jax.random.randint(seeds[2], (1,), 0, F - S + 1).astype(jnp.int32),
    }


def reference(frames, segments, offset):
    total = frames.shape[0]
    mean = jnp.sum(frames.astype(jnp.float32), axis=0) / total
    centered = (frames.astype(jnp.float32) - mean).astype(jnp.bfloat16)
    slab = lax.dynamic_slice_in_dim(centered, offset[0].astype(jnp.int32), S, 1)
    dims = (((0,), (0,)), ((), ()))
    instant = lax.dot_general(slab, centered, dims, preferred_element_type=jnp.float32) / total
    count = total - LAG
    valid = (segments[:count] == segments[LAG:]).astype(jnp.bfloat16)[:, None]
    pairs = jnp.sum(valid.astype(jnp.float32))
    left = jnp.concatenate([slab[:count], slab[LAG:]], axis=0)
    right = jnp.concatenate([centered[LAG:] * valid, centered[:count] * valid], axis=0)
    lagged = lax.dot_general(left, right, dims, preferred_element_type=jnp.float32) * 0.5 / pairs
    return instant, lagged
```

```python
import jax
import jax.numpy as jnp
from jax import lax
from jax.experimental import pallas as pl
from jax.experimental.pallas import tpu as pltpu
from jax.sharding import Mesh, PartitionSpec as P

S = 4096
LAG = 256
FRAMES = 1024
W = 768
ROWS = 1024
AXES = ("tm", "y", "x", "zl", "core")
TILE = ("y", "x", "zl", "core")
F32 = jnp.float32
BF16 = jnp.bfloat16


def shift(value, axis, size, step):
    return lax.ppermute(value, axis, [(i, (i + step) % size) for i in range(size)])


def swap(value, axis):
    return lax.ppermute(value, axis, [(0, 1), (1, 0)])


def columns_kernel(place, own, next_lo, next_hi, prev_lo, prev_hi, far_lo, far_hi, valid, c_out, r_out, c_all):
    total = jnp.sum(own[...].astype(F32), axis=0, keepdims=True)
    for ref in (next_lo, next_hi, prev_lo, prev_hi, far_lo, far_hi):
        total += jnp.sum(ref[...].astype(F32), axis=0, keepdims=True)
    mean = total * (1.0 / FRAMES)
    c_all[0] = (own[...].astype(F32) - mean).astype(BF16)
    for d, lo, hi in ((1, next_lo, next_hi), (2, far_lo, far_hi), (3, prev_lo, prev_hi)):
        c_all[d, :128] = (lo[...].astype(F32) - mean).astype(BF16)
        c_all[d, 128:] = (hi[...].astype(F32) - mean).astype(BF16)
    for dc in range(2):
        for dy in range(4):
            core = lax.rem(place[1] + dc, 2)
            y = lax.rem(place[0] + dy, 4)
            rows = pl.ds(pl.multiple_of(core * 128 + y * 32, 32), 32)
            for d in range(4):
                c_out[dc, dy, d] = c_all[d, rows, :]
                after = c_all[(d + 1) % 4, rows, :].astype(F32) * valid[d, rows, :]
                before = c_all[(d + 3) % 4, rows, :].astype(F32) * valid[(d + 3) % 4, rows, :]
                r_out[dc, dy, d] = (after + before).astype(BF16)


def product_kernel(scale, *refs):
    slabs, c, r, instant, lagged, held = refs[:8], refs[8], refs[9], refs[10], refs[11], refs[12]
    total = jnp.zeros((1, held.shape[-1]), F32)
    for ref in slabs:
        total += jnp.sum(ref[...].astype(F32).reshape(128, -1), axis=0, keepdims=True)
    mean = total * (1.0 / FRAMES)
    for n, ref in enumerate(slabs):
        held[128 * n : 128 * n + 128] = (ref[...].reshape(128, -1).astype(F32) - mean).astype(BF16)
    dims = (((0,), (0,)), ((), ()))
    left = held[...]
    instant[...] = lax.dot_general(left, c[...], dims, preferred_element_type=F32) * (1.0 / FRAMES)
    lagged[...] = lax.dot_general(left, r[...], dims, preferred_element_type=F32) * scale[0]


def shards(frames, segments, offset):
    tm, y, x = lax.axis_index("tm"), lax.axis_index("y"), lax.axis_index("x")
    zl, core = lax.axis_index("zl"), lax.axis_index("core")
    start = offset[0]

    order = ("core", "y", "x", "zl")
    spread = lax.all_to_all(frames.reshape(64, 4, W), order, 0, 0, tiled=True).reshape(2, 32, 4, W)
    pair = jnp.minimum(start // (2 * W), 28)
    mine = lax.dynamic_slice(spread, (0, pair, 0, 0), (2, 4, 4, W))
    mine = mine.transpose(2, 1, 0, 3).reshape(4, 8 * W)
    mine = lax.dynamic_slice(mine, (0, start - pair * 2 * W), (4, S))

    lo, hi = frames[:128], frames[128:]
    prev_hi = shift(hi, "tm", 4, 1)
    next_lo = shift(lo, "tm", 4, -1)
    prev_lo = shift(lo, "tm", 4, 1)
    next_hi = shift(hi, "tm", 4, -1)
    far_hi = shift(prev_hi, "tm", 4, 1)
    far_lo = shift(next_lo, "tm", 4, -1)

    def block(d):
        return lax.dynamic_slice(mine, (0, lax.rem(tm + d, 4) * ROWS), (4, ROWS))

    got = [block(0)] + [shift(block(4 - d), "tm", 4, 4 - d) for d in (1, 2, 3)]
    part = jnp.stack(got)
    other = swap(part, "zl")
    first = zl == 0
    part = jnp.concatenate([jnp.where(first, part, other), jnp.where(first, other, part)], axis=1)
    rel = [part] + [shift(part, "x", 4, 4 - d) for d in (1, 2, 3)]
    nat = []
    for i in range(4):
        d = lax.rem(i - x + 4, 4)
        nat.append(jnp.where(d == 0, rel[0], jnp.where(d == 1, rel[1], jnp.where(d == 2, rel[2], rel[3]))))
    part = jnp.concatenate(nat, axis=1)
    own = [part] + [shift(part, "y", 4, 4 - d) for d in (1, 2, 3)]
    slabs = own + [swap(p, "core") for p in own]

    blocks = segments.reshape(4, LAG)
    valid = jnp.concatenate([blocks[:3] == blocks[1:], jnp.zeros((1, LAG), jnp.bool_)]).astype(F32)
    scale = (0.5 / jnp.sum(valid)).reshape(1)
    valid = lax.dynamic_slice(jnp.concatenate([valid, valid]), (tm, 0), (4, LAG))[:, :, None]

    vmem = pl.BlockSpec(memory_space=pltpu.VMEM)
    smem = pl.BlockSpec(memory_space=pltpu.SMEM)
    c, r = pl.pallas_call(
        columns_kernel,
        out_shape=[jax.ShapeDtypeStruct((2, 4, 4, 32, W), BF16)] * 2,
        in_specs=[smem] + [vmem] * 8,
        out_specs=[vmem] * 2,
        scratch_shapes=[pltpu.VMEM((4, LAG, W), BF16)],
        compiler_params=pltpu.CompilerParams(vmem_limit_bytes=24 * 2**20),
        cost_estimate=pl.CostEstimate(flops=10**7, bytes_accessed=6 * 2**20, transcendentals=0),
        name="columns",
    )(jnp.stack([y, core]), frames, next_lo, next_hi, prev_lo, prev_hi, far_lo, far_hi, valid)
    c, r = c.reshape(FRAMES, W), r.reshape(FRAMES, W)

    tile = 256
    outs = pl.pallas_call(
        product_kernel,
        grid=(ROWS // tile,),
        out_shape=[jax.ShapeDtypeStruct((ROWS, W), F32)] * 2,
        in_specs=[smem]
        + [pl.BlockSpec((4, 32, tile), lambda i: (0, 0, i))] * 8
        + [pl.BlockSpec((FRAMES, W), lambda i: (0, 0))] * 2,
        out_specs=[pl.BlockSpec((tile, W), lambda i: (i, 0))] * 2,
        scratch_shapes=[pltpu.VMEM((FRAMES, tile), BF16)],
        compiler_params=pltpu.CompilerParams(vmem_limit_bytes=32 * 2**20),
        cost_estimate=pl.CostEstimate(flops=4 * FRAMES * ROWS * W, bytes_accessed=12 * 2**20, transcendentals=0),
        name="products",
    )(scale, *slabs, c, r)
    return tuple(outs)


def solution(mesh):
    fine = Mesh(mesh.devices.reshape(4, 4, 4, 2, 2), AXES)
    cut = P("tm", TILE)
    return jax.shard_map(shards, mesh=fine, in_specs=(cut, P(), P()), out_specs=(cut, cut), check_vma=False)
```

```python
import functools

import jax
import jax.numpy as jnp
from jax import lax
from jax.experimental import pallas as pl
from jax.experimental.pallas import tpu as pltpu
from jax.sharding import Mesh, PartitionSpec as P

S = 4096
LAG = 256
FRAMES = 1024
W = 768
ROWS = 1024
HALF = 512
AXES = ("tm", "y", "x", "zl", "core")
TILE = ("y", "x", "zl", "core")
F32 = jnp.float32
BF16 = jnp.bfloat16


def shift(value, axis, size, step):
    return lax.ppermute(value, axis, [(i, (i + step) % size) for i in range(size)])


def swap(value, axis):
    return lax.ppermute(value, axis, [(0, 1), (1, 0)])


def columns_kernel(tm, own, next_, prev, far_lo, far_hi, valid, out, sums, held, sems):
    parts = ((own, held.at[0]), (next_, held.at[1]), (prev, held.at[3]), (far_lo, held.at[2, :128]), (far_hi, held.at[2, 128:]))
    copies = [pltpu.make_async_copy(a, b, sems.at[n]) for n, (a, b) in enumerate(parts)]
    for copy in copies:
        copy.start()
    for copy in copies:
        copy.wait()
    total = jnp.zeros((1, W), F32)
    for d in range(4):
        total += jnp.sum(held[d].astype(F32), axis=0, keepdims=True)
    mean = total * (1.0 / FRAMES)
    for d in range(4):
        held[d] = (held[d].astype(F32) - mean).astype(BF16)
    c_total = jnp.zeros((1, W), F32)
    r_total = jnp.zeros((1, W), F32)
    for d in range(4):
        j = lax.rem(tm[0] + d, 4)
        i = lax.rem(tm[0] + d + 3, 4)
        here = held[d]
        out[:, d, :, :W] = here.reshape(16, 16, W)
        c_total += jnp.sum(here.astype(F32), axis=0, keepdims=True)
        here = held[(d + 1) % 4].astype(F32) * valid[j] + held[(d + 3) % 4].astype(F32) * valid[i]
        here = here.astype(BF16)
        out[:, d, :, W:] = here.reshape(16, 16, W)
        r_total += jnp.sum(here.astype(F32), axis=0, keepdims=True)
    sums[:, :W] = c_total
    sums[:, W:] = r_total


def product_kernel(which, scale, slab, right, sums, *refs):
    instant, lagged = refs[-2:]
    left = slab[...].T
    mean = jnp.sum(left.astype(F32), axis=1, keepdims=True) * (1.0 / FRAMES)
    value = jnp.dot(left, right[:, :W], preferred_element_type=F32)
    instant[...] = (value - mean * sums[:, :W]) * (1.0 / FRAMES)
    value = jnp.dot(left, right[:, W:], preferred_element_type=F32)
    lagged[...] = (value - mean * sums[:, W:]) * scale[0]


def products(which, scale, slab, right, sums, before=()):
    tile = 256
    steps = HALF // tile
    return pl.pallas_call(
        product_kernel,
        grid_spec=pltpu.PrefetchScalarGridSpec(
            num_scalar_prefetch=1,
            grid=(steps,),
            in_specs=[pl.BlockSpec(memory_space=pltpu.SMEM)]
            + [pl.BlockSpec((FRAMES, tile), lambda i, w: (0, i))]
            + [pl.BlockSpec((FRAMES, 2 * W), lambda i, w: (0, 0))]
            + [pl.BlockSpec((1, 2 * W), lambda i, w: (0, 0))]
            + [pl.BlockSpec(memory_space=pl.ANY)] * len(before),
            out_specs=[pl.BlockSpec((tile, W), lambda i, w: (w[0] * steps + i, 0))] * 2,
        ),
        out_shape=[jax.ShapeDtypeStruct((ROWS, W), F32)] * 2,
        input_output_aliases={5: 0, 6: 1} if before else {},
        compiler_params=pltpu.CompilerParams(vmem_limit_bytes=20 * 2**20),
        cost_estimate=pl.CostEstimate(flops=4 * FRAMES * HALF * W, bytes_accessed=6 * 2**20, transcendentals=0),
        name="products",
    )(which, scale, slab, right, sums, *before)


def shards(frames, segments, offset):
    tm = lax.axis_index("tm")
    zl, core = lax.axis_index("zl"), lax.axis_index("core")
    start = offset[0]

    prev = shift(frames, "tm", 4, 1)
    next_ = shift(frames, "tm", 4, -1)

    blocks = segments.reshape(4, LAG)
    valid = jnp.concatenate([blocks[:3] == blocks[1:], jnp.zeros((1, LAG), jnp.bool_)]).astype(F32)
    scale = (0.5 / jnp.sum(valid)).reshape(1)
    valid = valid[:, :, None]
    place = tm.reshape(1)
    def pick(frames):
        spread = lax.all_to_all(frames.reshape(16, 16, W), ("y", "x"), 0, 0, tiled=True)
        first = jnp.minimum(start // (4 * W), 13)
        mine = lax.dynamic_slice(spread, (first, 0, 0), (3, 16, W))
        column = zl * 2 + core
        zero = jnp.zeros((16, W), BF16)
        row = []
        for p in range(3):
            row += [jnp.where(column == n, mine[p], zero) for n in range(4)]
        row = lax.dynamic_slice(jnp.concatenate(row, axis=1), (0, start - first * 4 * W), (16, S))
        row = row.reshape(16, 4, 2, HALF)
        even = core == 0
        keep = jnp.where(even, row[:, :, 0], row[:, :, 1])
        give = jnp.where(even, row[:, :, 1], row[:, :, 0])
        return keep + swap(give, "core")

    keep = lax.cond(start >= 0, pick, lambda frames: jnp.zeros((16, 4, HALF), BF16), frames)
    keep, prev, next_ = lax.optimization_barrier((keep, prev, next_))
    keep = keep + swap(keep, "zl")

    def block(d):
        return lax.dynamic_slice(keep, (0, lax.rem(tm + d, 4), 0), (16, 1, HALF)).reshape(16, HALF)

    got = {d: shift(block(4 - d), "tm", 4, 4 - d) for d in (2, 1, 3)}
    part = jnp.stack([block(0), got[1], got[2], got[3]])
    part, prev, next_, scale, valid, place = lax.optimization_barrier((part, prev, next_, scale, valid, place))
    far_hi = shift(prev[128:], "tm", 4, 1)
    far_lo = shift(next_[:128], "tm", 4, -1)
    part = jnp.broadcast_to(part.reshape(1, 64, HALF), (16, 64, HALF))
    own = lax.all_to_all(part, ("y", "x"), 0, 0, tiled=True).reshape(FRAMES, HALF)

    smem = pl.BlockSpec(memory_space=pltpu.SMEM)
    vmem = pl.BlockSpec(memory_space=pltpu.VMEM)
    right, sums = pl.pallas_call(
        columns_kernel,
        out_shape=[jax.ShapeDtypeStruct((16, 4, 16, 2 * W), BF16), jax.ShapeDtypeStruct((1, 2 * W), F32)],
        in_specs=[smem] + [pl.BlockSpec(memory_space=pltpu.HBM)] * 5 + [vmem],
        out_specs=[vmem] * 2,
        scratch_shapes=[pltpu.VMEM((4, LAG, W), BF16), pltpu.SemaphoreType.DMA((5,))],
        compiler_params=pltpu.CompilerParams(vmem_limit_bytes=16 * 2**20),
        cost_estimate=pl.CostEstimate(flops=10**7, bytes_accessed=6 * 2**20, transcendentals=0),
        name="columns",
    )(place, frames, next_, prev, far_lo, far_hi, valid)
    own, right, sums = lax.optimization_barrier((own, right, sums))
    other = swap(own, "core")
    right = right.reshape(FRAMES, 2 * W)

    outs = products(core.reshape(1), scale, own, right, sums)
    outs = products(1 - core.reshape(1), scale, other, right, sums, outs)
    return tuple(outs)


def solution(mesh):
    fine = Mesh(mesh.devices.reshape(4, 4, 4, 2, 2), AXES)
    cut = P("tm", TILE)
    return jax.shard_map(shards, mesh=fine, in_specs=(cut, P(), P()), out_specs=(cut, cut), check_vma=False)
```

```python
import functools

import jax
import jax.numpy as jnp
from jax import lax
from jax.experimental import pallas as pl
from jax.experimental.pallas import tpu as pltpu
from jax.sharding import Mesh, PartitionSpec as P

S = 4096
LAG = 256
FRAMES = 1024
W = 768
ROWS = 1024
HALF = 512
AXES = ("tm", "y", "x", "zl", "core")
TILE = ("y", "x", "zl", "core")
F32 = jnp.float32
BF16 = jnp.bfloat16


def shift(value, axis, size, step):
    return lax.ppermute(value, axis, [(i, (i + step) % size) for i in range(size)])


def swap(value, axis):
    return lax.ppermute(value, axis, [(0, 1), (1, 0)])


def columns_kernel(own, next_, prev, far_lo, far_hi, valid, c_out, r_out, sums, held, c_held, r_held, sems, out_sems):
    parts = ((own, held.at[0]), (next_, held.at[1]), (prev, held.at[3]), (far_lo, held.at[2, :128]), (far_hi, held.at[2, 128:]))
    copies = [pltpu.make_async_copy(a, b, sems.at[n]) for n, (a, b) in enumerate(parts)]
    for copy in copies:
        copy.start()
    total = jnp.zeros((1, W), F32)
    for n, block in ((0, 0), (1, 1), (2, 3)):
        copies[n].wait()
        total += jnp.sum(held[block].astype(F32), axis=0, keepdims=True)
    copies[3].wait()
    copies[4].wait()
    total += jnp.sum(held[2].astype(F32), axis=0, keepdims=True)
    mean = total * (1.0 / FRAMES)
    outs = []
    c_total = jnp.zeros((1, W), F32)
    for d in range(4):
        value = (held[d].astype(F32) - mean).astype(BF16)
        c_held[d] = value.reshape(16, 16, W)
        c_total += jnp.sum(value.astype(F32), axis=0, keepdims=True)
        outs.append(pltpu.make_async_copy(c_held.at[d], c_out.at[:, d], out_sems.at[d]))
        outs[-1].start()
    weight = valid[...].T
    r_total = jnp.zeros((1, W), F32)
    for d in range(4):
        e, f = (d + 1) % 4, (d + 3) % 4
        after = c_held[e].reshape(LAG, W).astype(F32) * weight[:, d : d + 1]
        before = c_held[f].reshape(LAG, W).astype(F32) * weight[:, f : f + 1]
        value = (after + before).astype(BF16)
        r_held[d] = value.reshape(16, 16, W)
        r_total += jnp.sum(value.astype(F32), axis=0, keepdims=True)
        outs.append(pltpu.make_async_copy(r_held.at[d], r_out.at[:, d], out_sems.at[4 + d]))
        outs[-1].start()
    sums[:1] = c_total
    sums[1:] = r_total
    for copy in outs:
        copy.wait()


def product_kernel(which, scale, slab, c, r, sums, *refs):
    instant, lagged = refs[-2:]
    left = slab[...].T
    mean = jnp.sum(left.astype(F32), axis=1, keepdims=True) * (1.0 / FRAMES)
    value = jnp.dot(left, c[...], preferred_element_type=F32)
    instant[...] = (value - mean * sums[:1]) * (1.0 / FRAMES)
    value = jnp.dot(left, r[...], preferred_element_type=F32)
    lagged[...] = (value - mean * sums[1:]) * scale[0]


def products(which, scale, slab, c, r, sums, before=()):
    tile = 256
    steps = HALF // tile
    return pl.pallas_call(
        product_kernel,
        grid_spec=pltpu.PrefetchScalarGridSpec(
            num_scalar_prefetch=1,
            grid=(steps,),
            in_specs=[
                pl.BlockSpec(memory_space=pltpu.SMEM),
                pl.BlockSpec((FRAMES, tile), lambda i, w: (0, i)),
                pl.BlockSpec((FRAMES, W), lambda i, w: (0, 0)),
                pl.BlockSpec((FRAMES, W), lambda i, w: (0, 0)),
                pl.BlockSpec((2, W), lambda i, w: (0, 0)),
            ]
            + [pl.BlockSpec(memory_space=pl.ANY)] * len(before),
            out_specs=[pl.BlockSpec((tile, W), lambda i, w: (w[0] * steps + i, 0))] * 2,
        ),
        out_shape=[jax.ShapeDtypeStruct((ROWS, W), F32)] * 2,
        input_output_aliases={6: 0, 7: 1} if before else {},
        compiler_params=pltpu.CompilerParams(vmem_limit_bytes=20 * 2**20),
        cost_estimate=pl.CostEstimate(flops=4 * FRAMES * HALF * W, bytes_accessed=6 * 2**20, transcendentals=0),
        name="products",
    )(which, scale, slab, c, r, sums, *before)


def shards(frames, segments, offset):
    tm = lax.axis_index("tm")
    zl, core = lax.axis_index("zl"), lax.axis_index("core")
    start = offset[0]

    prev = shift(frames, "tm", 4, 1)
    next_ = shift(frames, "tm", 4, -1)

    blocks = segments.reshape(4, LAG)
    valid = jnp.concatenate([blocks[:3] == blocks[1:], jnp.zeros((1, LAG), jnp.bool_)]).astype(F32)
    scale = (0.5 / jnp.sum(valid)).reshape(1)
    valid = lax.dynamic_slice(jnp.concatenate([valid, valid, valid]), (tm, 0), (8, LAG))
    def pick(frames):
        spread = lax.all_to_all(frames.reshape(16, 16, W), ("y", "x"), 0, 0, tiled=True)
        first = jnp.minimum(start // (4 * W), 13)
        mine = lax.dynamic_slice(spread, (first, 0, 0), (3, 16, W))
        column = zl * 2 + core
        zero = jnp.zeros((16, W), BF16)
        row = []
        for p in range(3):
            row += [jnp.where(column == n, mine[p], zero) for n in range(4)]
        row = lax.dynamic_slice(jnp.concatenate(row, axis=1), (0, start - first * 4 * W), (16, S))
        row = row.reshape(16, 4, 2, HALF)
        even = core == 0
        keep = jnp.where(even, row[:, :, 0], row[:, :, 1])
        give = jnp.where(even, row[:, :, 1], row[:, :, 0])
        return keep + swap(give, "core")

    keep = lax.cond(start >= 0, pick, lambda frames: jnp.zeros((16, 4, HALF), BF16), frames)
    keep, prev, next_ = lax.optimization_barrier((keep, prev, next_))
    keep = keep + swap(keep, "zl")

    def block(d):
        return lax.dynamic_slice(keep, (0, lax.rem(tm + d, 4), 0), (16, 1, HALF)).reshape(16, HALF)

    got = {d: shift(block(4 - d), "tm", 4, 4 - d) for d in (2, 1, 3)}
    part = jnp.stack([block(0), got[1], got[2], got[3]])
    part, prev, next_, scale, valid = lax.optimization_barrier((part, prev, next_, scale, valid))
    far_hi = shift(prev[128:], "tm", 4, 1)
    far_lo = shift(next_[:128], "tm", 4, -1)
    part = jnp.broadcast_to(part.reshape(1, 64, HALF), (16, 64, HALF))
    own = lax.all_to_all(part, ("y", "x"), 0, 0, tiled=True).reshape(FRAMES, HALF)

    smem = pl.BlockSpec(memory_space=pltpu.SMEM)
    vmem = pl.BlockSpec(memory_space=pltpu.VMEM)
    c, r, sums = pl.pallas_call(
        columns_kernel,
        out_shape=[jax.ShapeDtypeStruct((16, 4, 16, W), BF16)] * 2 + [jax.ShapeDtypeStruct((2, W), F32)],
        in_specs=[pl.BlockSpec(memory_space=pl.ANY)] * 5 + [vmem],
        out_specs=[pl.BlockSpec(memory_space=pl.ANY)] * 2 + [vmem],
        scratch_shapes=[pltpu.VMEM((4, LAG, W), BF16)]
        + [pltpu.VMEM((4, 16, 16, W), BF16)] * 2
        + [pltpu.SemaphoreType.DMA((5,)), pltpu.SemaphoreType.DMA((8,))],
        compiler_params=pltpu.CompilerParams(vmem_limit_bytes=12 * 2**20),
        cost_estimate=pl.CostEstimate(flops=10**7, bytes_accessed=6 * 2**20, transcendentals=0),
        name="columns",
    )(frames, next_, prev, far_lo, far_hi, valid)
    own, c, r, sums = lax.optimization_barrier((own, c, r, sums))
    other = swap(own, "core")
    c, r = c.reshape(FRAMES, W), r.reshape(FRAMES, W)

    outs = products(core.reshape(1), scale, own, c, r, sums)
    outs = products(1 - core.reshape(1), scale, other, c, r, sums, outs)
    return tuple(outs)


def solution(mesh):
    fine = Mesh(mesh.devices.reshape(4, 4, 4, 2, 2), AXES)
    cut = P("tm", TILE)
    return jax.shard_map(shards, mesh=fine, in_specs=(cut, P(), P()), out_specs=(cut, cut), check_vma=False)
```

```python
import functools

import jax
import jax.numpy as jnp
from jax import lax
from jax.experimental import pallas as pl
from jax.experimental.pallas import tpu as pltpu
from jax.sharding import Mesh, PartitionSpec as P

S = 4096
LAG = 256
FRAMES = 1024
W = 768
ROWS = 1024
HALF = 512
AXES = ("tm", "y", "x", "zl", "core")
TILE = ("y", "x", "zl", "core")
F32 = jnp.float32
BF16 = jnp.bfloat16


def shift(value, axis, size, step):
    return lax.ppermute(value, axis, [(i, (i + step) % size) for i in range(size)])


def swap(value, axis):
    return lax.ppermute(value, axis, [(0, 1), (1, 0)])


def columns_kernel(own, next_, prev, far_lo, far_hi, valid, c_out, r_out, sums, held, c_held, r_held, sems, out_sems):
    parts = ((own, held.at[0]), (next_, held.at[1]), (prev, held.at[3]), (far_lo, held.at[2, :128]), (far_hi, held.at[2, 128:]))
    copies = [pltpu.make_async_copy(a, b, sems.at[n]) for n, (a, b) in enumerate(parts)]
    for copy in copies:
        copy.start()
    total = jnp.zeros((1, W), F32)
    for n, block in ((0, 0), (1, 1), (2, 3)):
        copies[n].wait()
        total += jnp.sum(held[block].astype(F32), axis=0, keepdims=True)
    copies[3].wait()
    copies[4].wait()
    total += jnp.sum(held[2].astype(F32), axis=0, keepdims=True)
    mean = total * (1.0 / FRAMES)
    outs = []
    c_total = jnp.zeros((1, W), F32)
    for d in range(4):
        value = (held[d].astype(F32) - mean).astype(BF16)
        for g in range(16):
            c_held[d, g % 4 * 4 + g // 4] = value[16 * g : 16 * g + 16]
        c_total += jnp.sum(value.astype(F32), axis=0, keepdims=True)
        outs.append(pltpu.make_async_copy(c_held.at[d], c_out.at[:, d], out_sems.at[d]))
        outs[-1].start()
    weight = valid[...].T
    r_total = jnp.zeros((1, W), F32)
    for d in range(4):
        e, f = (d + 1) % 4, (d + 3) % 4
        after = c_held[e].reshape(LAG, W).astype(F32) * weight[:, d : d + 1]
        before = c_held[f].reshape(LAG, W).astype(F32) * weight[:, f : f + 1]
        value = (after + before).astype(BF16)
        r_held[d] = value.reshape(16, 16, W)
        r_total += jnp.sum(value.astype(F32), axis=0, keepdims=True)
        outs.append(pltpu.make_async_copy(r_held.at[d], r_out.at[:, d], out_sems.at[4 + d]))
        outs[-1].start()
    sums[:1] = c_total
    sums[1:] = r_total
    for copy in outs:
        copy.wait()


def product_kernel(which, scale, slab, c, r, sums, *refs):
    instant, lagged = refs[-2:]
    left = slab[...].T
    mean = jnp.sum(left.astype(F32), axis=1, keepdims=True) * (1.0 / FRAMES)
    value = jnp.dot(left, c[...], preferred_element_type=F32)
    instant[...] = (value - mean * sums[:1]) * (1.0 / FRAMES)
    value = jnp.dot(left, r[...], preferred_element_type=F32)
    lagged[...] = (value - mean * sums[1:]) * scale[0]


def products(which, scale, slab, c, r, sums, before=()):
    tile = 256
    steps = HALF // tile
    return pl.pallas_call(
        product_kernel,
        grid_spec=pltpu.PrefetchScalarGridSpec(
            num_scalar_prefetch=1,
            grid=(steps,),
            in_specs=[
                pl.BlockSpec(memory_space=pltpu.SMEM),
                pl.BlockSpec((FRAMES, tile), lambda i, w: (0, i)),
                pl.BlockSpec((FRAMES, W), lambda i, w: (0, 0)),
                pl.BlockSpec((FRAMES, W), lambda i, w: (0, 0)),
                pl.BlockSpec((2, W), lambda i, w: (0, 0)),
            ]
            + [pl.BlockSpec(memory_space=pl.ANY)] * len(before),
            out_specs=[pl.BlockSpec((tile, W), lambda i, w: (w[0] * steps + i, 0))] * 2,
        ),
        out_shape=[jax.ShapeDtypeStruct((ROWS, W), F32)] * 2,
        input_output_aliases={6: 0, 7: 1} if before else {},
        compiler_params=pltpu.CompilerParams(vmem_limit_bytes=20 * 2**20),
        cost_estimate=pl.CostEstimate(flops=4 * FRAMES * HALF * W, bytes_accessed=6 * 2**20, transcendentals=0),
        name="products",
    )(which, scale, slab, c, r, sums, *before)


def shards(frames, segments, offset):
    tm = lax.axis_index("tm")
    zl, core = lax.axis_index("zl"), lax.axis_index("core")
    start = offset[0]

    prev = shift(frames, "tm", 4, 1)
    next_ = shift(frames, "tm", 4, -1)

    blocks = segments.reshape(4, LAG)
    valid = jnp.concatenate([blocks[:3] == blocks[1:], jnp.zeros((1, LAG), jnp.bool_)]).astype(F32)
    scale = (0.5 / jnp.sum(valid)).reshape(1)
    valid = lax.dynamic_slice(jnp.concatenate([valid, valid, valid]), (tm, 0), (8, LAG))
    valid = valid.reshape(8, 4, 4, 16).transpose(0, 2, 1, 3).reshape(8, LAG)
    def pick(frames):
        spread = lax.all_to_all(frames.reshape(16, 16, W), ("y", "x"), 0, 0, tiled=True)
        first = jnp.minimum(start // (4 * W), 13)
        mine = lax.dynamic_slice(spread, (first, 0, 0), (3, 16, W))
        column = zl * 2 + core
        zero = jnp.zeros((16, W), BF16)
        row = []
        for p in range(3):
            row += [jnp.where(column == n, mine[p], zero) for n in range(4)]
        row = lax.dynamic_slice(jnp.concatenate(row, axis=1), (0, start - first * 4 * W), (16, S))
        row = row.reshape(16, 4, 2, HALF)
        even = core == 0
        keep = jnp.where(even, row[:, :, 0], row[:, :, 1])
        give = jnp.where(even, row[:, :, 1], row[:, :, 0])
        return keep + swap(give, "core")

    keep = lax.cond(start >= 0, pick, lambda frames: jnp.zeros((16, 4, HALF), BF16), frames)
    keep, prev, next_ = lax.optimization_barrier((keep, prev, next_))
    keep = keep + swap(keep, "zl")

    def block(d):
        return lax.dynamic_slice(keep, (0, lax.rem(tm + d, 4), 0), (16, 1, HALF)).reshape(16, HALF)

    got = {d: shift(block(4 - d), "tm", 4, 4 - d) for d in (2, 1, 3)}
    part = jnp.stack([block(0), got[1], got[2], got[3]])
    part, prev, next_, scale, valid = lax.optimization_barrier((part, prev, next_, scale, valid))
    far_hi = shift(prev[128:], "tm", 4, 1)
    far_lo = shift(next_[:128], "tm", 4, -1)
    part = jnp.broadcast_to(part.reshape(1, 64, HALF), (16, 64, HALF))
    own = lax.all_to_all(part, ("x", "y"), 0, 0, tiled=True).reshape(FRAMES, HALF)

    smem = pl.BlockSpec(memory_space=pltpu.SMEM)
    vmem = pl.BlockSpec(memory_space=pltpu.VMEM)
    c, r, sums = pl.pallas_call(
        columns_kernel,
        out_shape=[jax.ShapeDtypeStruct((16, 4, 16, W), BF16)] * 2 + [jax.ShapeDtypeStruct((2, W), F32)],
        in_specs=[pl.BlockSpec(memory_space=pl.ANY)] * 5 + [vmem],
        out_specs=[pl.BlockSpec(memory_space=pl.ANY)] * 2 + [vmem],
        scratch_shapes=[pltpu.VMEM((4, LAG, W), BF16)]
        + [pltpu.VMEM((4, 16, 16, W), BF16)] * 2
        + [pltpu.SemaphoreType.DMA((5,)), pltpu.SemaphoreType.DMA((8,))],
        compiler_params=pltpu.CompilerParams(vmem_limit_bytes=12 * 2**20),
        cost_estimate=pl.CostEstimate(flops=10**7, bytes_accessed=6 * 2**20, transcendentals=0),
        name="columns",
    )(frames, next_, prev, far_lo, far_hi, valid)
    own, c, r, sums = lax.optimization_barrier((own, c, r, sums))
    other = swap(own, "core")
    c, r = c.reshape(FRAMES, W), r.reshape(FRAMES, W)

    outs = products(core.reshape(1), scale, own, c, r, sums)
    outs = products(1 - core.reshape(1), scale, other, c, r, sums, outs)
    return tuple(outs)


def solution(mesh):
    fine = Mesh(mesh.devices.reshape(4, 4, 4, 2, 2), AXES)
    cut = P("tm", TILE)
    return jax.shard_map(shards, mesh=fine, in_specs=(cut, P(), P()), out_specs=(cut, cut), check_vma=False)
```
